256 devices in a mesh: section: 16 (over z_lo, y, core), peer: 16 (over z_hi, x).
Axes of the slice: x: 4, y: 4, z: 8 (z_hi: 4, z_lo: 2; z = z_hi * 2 + z_lo), core: 2. Of those that a mesh axis runs over, the one named last changes fastest.
Arguments:
- hidden: bfloat16 [8192, 2048], P(('section', 'peer')), may hold values from -6 to 6
- up_weight: bfloat16 [16, 2048, 8192], P('section', None, 'peer'), may hold values from -0.125 to 0.125
- down_weight: bfloat16 [16, 8192, 2048], P('section', 'peer'), may hold values from -0.0625 to 0.0625
- matching: int32 [16, 16, 1], replicated, may hold values from 0 to 15; in each aligned block of 16 rows (0 to 15, 16 to 31, ..., all dimensions but the last counted through in order) at most 2 rows name the same one
- cotangent: bfloat16 [16, 1024, 2048], P('section', 'peer'), may hold values from -6 to 6
Outputs:
- grad_up: bfloat16 [16, 2048, 8192], P('section', None, 'peer')
- grad_down: bfloat16 [16, 8192, 2048], P('section', 'peer')
- input_grad: bfloat16 [8192, 2048], P(('section', 'peer'))
The draws below stay inside these ranges and needn't reach their ends.
Inputs may be any that keep to these rules, and one draw needn't show every extreme that they name: matching[s, p, 0] names the peer of section (s + 1) mod the number of sections that takes peer p's micro-batch; within one section no peer is named more than 2 times, a bound that some block reaches.
All inputs are finite; a program needn't handle non-finite values.
Results may differ from the reference program's by a relative error of at most 0.023.
Values may be sent and summed in bfloat16 or wider, within the bound.
No kernel may reach another device: no remote copies, remote signals or barrier semaphores. Data moves between devices by JAX's collectives and lax.ppermute only.
A program may use at most 128 MiB of HBM per device.

```python
import math
import jax
import jax.numpy as jnp
import numpy as np
from jax import lax

D = 2048
FF = 8192
TOK_DEV = 32
MOST = 2
GROUP = 512
TOKENS = 8192
N_SECTION = 16
N_PEER = 16


def levels(own_key, shape, cuts, low, high):
    level = 1.0
    for position, shards_of in cuts:
        heights = jax.random.uniform(jax.random.fold_in(jax.random.fold_in(own_key, 6), position), (shards_of,), jnp.float32, low / len(cuts), high / len(cuts))
        level = level * jnp.repeat(jnp.exp(heights), shape[position] // shards_of).reshape((-1,) + (1,) * (len(shape) - 1 - position))
    return level


def deal_out(own_key, own, number, rows, number_of, top, most, lean):
    sequence = jax.random.permutation(own_key, number_of)
    packed, ordinary = shares(number_of, rows * top, most, lean, True), shares(number_of, rows * top, most, lean, False)
    places = jnp.arange(number_of)

    def named(tallies, turn):
        used = int((tallies > 0).sum())
        fixed = max(1, used // 4)
        moved = fixed + (places - fixed + turn * (used - fixed)) % max(1, number_of - fixed)
        return jnp.zeros((number_of,), jnp.int32).at[sequence[jnp.where(places < fixed, places, moved)]].set(jnp.asarray(tallies, jnp.int32))

    tallies = jnp.where(number % 4 == 0, named(packed, number // 4), named(ordinary, number - number // 4 - 1))
    mixed = jax.random.permutation(jax.random.fold_in(own, 3), number_of)
    donor, taker = mixed[0:number_of // 2 * 2:2], mixed[1:number_of // 2 * 2:2]
    slack = jnp.minimum(tallies[donor] - 1, most - tallies[taker]) // 2
    slack = jnp.where((donor == sequence[0]) | (taker == sequence[0]) | (tallies[taker] == 0), 0, jnp.maximum(slack, 0))
    moved = jax.random.randint(jax.random.fold_in(own, 4), (number_of // 2,), 0, 1 << 20) % (slack + 1)
    tallies = tallies.at[donor].add(-moved).at[taker].add(moved)
    members = jnp.searchsorted(jnp.cumsum(tallies), jnp.arange(rows * top), side="right").astype(jnp.int32)
    table = members.reshape(top, rows).T
    table = table[jax.random.permutation(jax.random.fold_in(own, 1), rows)]
    turn = jax.random.randint(jax.random.fold_in(own, 2), (rows, 1), 0, top)
    return jnp.take_along_axis(table, (jnp.arange(top)[None, :] + turn) % top, axis=1)


def shares(number_of, total, bound, slope, full):
    portions = [(1 << 20) // math.isqrt(grade ** slope) + 1 for grade in range(1, number_of + 1)]
    largest = bound if full else min(bound, max(-(-total // number_of), total * portions[0] // sum(portions)))
    least = 1 if total - largest >= number_of - 1 else 0
    counts, surplus = [largest] + [least] * (number_of - 1), total - largest - least * (number_of - 1)
    while surplus > 0:
        movable = [i for i in range(1, number_of) if counts[i] < largest] or [i for i in range(1, number_of) if counts[i] < bound]
        mass, remaining = sum([portions[i] for i in movable]), surplus
        for i in movable:
            addition = min(bound - counts[i], max(1, remaining * portions[i] // mass), surplus)
            counts[i] = counts[i] + addition
            surplus = surplus - addition
    return np.array(counts)


def centred(key, dims, deviation, limit, shards=(), held_as=jnp.bfloat16):
    result = jax.random.normal(key, dims, jnp.float32) * deviation
    if len(shards) > 0:
        result = levels(key, dims, shards, -0.22, 0.18) * result
    return jnp.clip(result, min=-limit, max=limit).astype(held_as)


def setup_inputs(seed: int = 0) -> dict:
    splits = jax.random.split(jax.random.key(seed), 6)
    hidden = centred(splits[0], (TOKENS, D), 1.0, 6.0, ((0, 256),))
    up_weight = centred(splits[1], (N_SECTION, D, FF), D ** -0.5, 0.125, ((0, 16), (2, 16)))
    down_weight = centred(splits[2], (N_SECTION, FF, D), FF ** -0.5, 0.0625, ((0, 16), (1, 16)))
    matching_keys = jax.random.split(jax.random.fold_in(splits[3], 1), N_SECTION * N_PEER // N_PEER)
    matching_turns = jax.random.permutation(jax.random.fold_in(splits[3], 3), N_SECTION * N_PEER // N_PEER)
    matching = jax.vmap(lambda own, number: deal_out(jax.random.fold_in(splits[3], 2), own, number, N_PEER, N_PEER, 1, MOST, 2))(matching_keys, matching_turns).reshape((N_SECTION, N_PEER, 1))
    cotangent = centred(splits[4], (N_SECTION, N_PEER * MOST * TOK_DEV, D), 1.0, 6.0, ((0, 16), (1, 16)))
    return {"hidden": hidden, "up_weight": up_weight, "down_weight": down_weight, "matching": matching, "cotangent": cotangent}


epsilon = 1e-06
gelu_scale = math.sqrt(2.0 / math.pi)
cubic_coef = 0.044715

def normalize(values):
    wide = values.astype(jnp.float32)
    radius = jnp.sqrt(lax.optimization_barrier(jnp.mean(wide * wide, axis=-1, keepdims=True)) + epsilon)
    return (wide / radius, radius)

def norm_back(unit_rows, radius, grad_rows):
    inner = lax.optimization_barrier(jnp.mean(grad_rows * unit_rows, axis=-1, keepdims=True))
    return (grad_rows - unit_rows * inner) / radius

def gelu_value(pre):
    tangent = jnp.tanh(gelu_scale * (pre + cubic_coef * pre * pre * pre))
    return 0.5 * pre * (1.0 + tangent)

def gelu_slope(pre):
    tangent = jnp.tanh(gelu_scale * (pre + cubic_coef * pre * pre * pre))
    return 0.5 * (1.0 + tangent) + 0.5 * pre * (1.0 - tangent * tangent) * gelu_scale * (1.0 + 3.0 * cubic_coef * pre * pre)

def forward_section(section_in):
    rows_in, up_mat, down_mat = section_in
    unit_rows, radius = normalize(rows_in)
    norm_rows = unit_rows.astype(jnp.bfloat16)
    pre = jnp.dot(norm_rows, up_mat, preferred_element_type=jnp.float32)
    act = gelu_value(pre).astype(jnp.bfloat16)
    out_rows = rows_in.astype(jnp.float32) + jnp.dot(act, down_mat, preferred_element_type=jnp.float32)
    return out_rows.astype(jnp.bfloat16)

def second_section(section_in):
    moved, target, up_mat, down_mat = section_in
    unit_rows, radius = normalize(moved)
    norm_rows = unit_rows.astype(jnp.bfloat16)
    pre = jnp.dot(norm_rows, up_mat, preferred_element_type=jnp.float32)
    act = gelu_value(pre).astype(jnp.bfloat16)
    slope_in = jnp.dot(target, down_mat.T, preferred_element_type=jnp.float32)
    grad_pre = (slope_in * gelu_slope(pre)).astype(jnp.bfloat16)
    up_part = jnp.dot(norm_rows.T, grad_pre, preferred_element_type=jnp.float32)
    down_part = jnp.dot(act.T, target, preferred_element_type=jnp.float32)
    back_norm = jnp.dot(grad_pre, up_mat.T, preferred_element_type=jnp.float32)
    moved_grad = (target.astype(jnp.float32) + norm_back(unit_rows, radius, back_norm)).astype(jnp.bfloat16)
    return (moved_grad, up_part, down_part)

def first_back_section(section_in):
    rows_in, back, up_mat, down_mat, up_part, down_part = section_in
    unit_rows, radius = normalize(rows_in)
    norm_rows = unit_rows.astype(jnp.bfloat16)
    pre = jnp.dot(norm_rows, up_mat, preferred_element_type=jnp.float32)
    act = gelu_value(pre).astype(jnp.bfloat16)
    slope_in = jnp.dot(back, down_mat.T, preferred_element_type=jnp.float32)
    grad_pre = (slope_in * gelu_slope(pre)).astype(jnp.bfloat16)
    up_total = up_part + jnp.dot(norm_rows.T, grad_pre, preferred_element_type=jnp.float32)
    down_total = down_part + jnp.dot(act.T, back, preferred_element_type=jnp.float32)
    back_norm = jnp.dot(grad_pre, up_mat.T, preferred_element_type=jnp.float32)
    input_rows = (back.astype(jnp.float32) + norm_back(unit_rows, radius, back_norm)).astype(jnp.bfloat16)
    return (up_total.astype(jnp.bfloat16), down_total.astype(jnp.bfloat16), input_rows)

def pick_slots(slot_blocks, slot_index):
    return jnp.take(slot_blocks, slot_index, axis=0)

def reference(hidden, up_weight, down_weight, matching, cotangent):
    sectioned = hidden.reshape(N_SECTION, GROUP, D)
    section_out = lax.map(forward_section, (sectioned, up_weight, down_weight))
    moved = jnp.roll(section_out, 1, axis=0)
    prev_match = jnp.roll(matching[:, :, 0], 1, axis=0).astype(jnp.int32)
    same_dest = prev_match[:, :, None] == prev_match[:, None, :]
    peer_line = jnp.arange(N_PEER, dtype=jnp.int32)
    earlier = peer_line[None, :] < peer_line[:, None]
    arrival_rank = lax.optimization_barrier(jnp.sum((same_dest & earlier[None]).astype(jnp.int32), axis=2)).astype(jnp.int32)
    slot_index = (prev_match * MOST + arrival_rank).astype(jnp.int32)
    slot_blocks = cotangent.reshape(N_SECTION, N_PEER * MOST, TOK_DEV, D)
    target = jax.vmap(pick_slots)(slot_blocks, slot_index).reshape(N_SECTION, GROUP, D)
    moved_grad, up_second, down_second = lax.map(second_section, (moved, target, up_weight, down_weight))
    back = jnp.roll(moved_grad, -1, axis=0)
    grad_up, grad_down, input_rows = lax.map(first_back_section, (sectioned, back, up_weight, down_weight, up_second, down_second))
    return (grad_up, grad_down, input_rows.reshape(TOKENS, D))
```

```python
import math

import jax
import jax.numpy as jnp
from jax import lax
from jax.sharding import PartitionSpec as P

epsilon = 1e-06
gelu_scale = math.sqrt(2.0 / math.pi)
cubic_coef = 0.044715
side = 4
chains = 1


def send(block, sections, deep, across):
    peers = lax.axis_size("peer")
    count = lax.axis_size("section")
    if sections == 0:
        route = [
            (p, (p // side + deep) % side * side + (p % side + across) % side)
            for p in range(peers)
        ]
        return lax.ppermute(block, "peer", route)
    route = [
        (
            s * peers + p,
            (s + sections) % count * peers
            + (p // side + deep) % side * side
            + (p % side + across) % side,
        )
        for s in range(count)
        for p in range(peers)
    ]
    return lax.ppermute(block, ("section", "peer"), route)


def gather_deep(block, sections=0):
    parts = [block if i == 0 and sections == 0 else send(block, sections, i, 0) for i in range(side)]
    return parts


def gather_across(group):
    half = group.shape[0] // 2
    after = send(group, 0, 0, 1)
    before = send(group, 0, 0, -1)
    far_low = send(after[:half], 0, 0, 1)
    far_high = send(before[half:], 0, 0, -1)
    return jnp.concatenate([group, after, far_low, far_high, before], axis=0)


def wide(values):
    return values.astype(jnp.float32)


def narrow(values):
    return values.astype(jnp.bfloat16)


def scatter_across(rows):
    quarter = rows.shape[0] // side
    half = quarter // 2
    own, near, far, last = [rows[j * quarter : (j + 1) * quarter] for j in range(side)]
    low = send(far[:half], 0, 0, -1)
    high = send(far[half:], 0, 0, 1)
    near = jnp.concatenate([narrow(wide(near[:half]) + wide(low)), near[half:]], axis=0)
    last = jnp.concatenate([last[:half], narrow(wide(last[half:]) + wide(high))], axis=0)
    near = send(near, 0, 0, -1)
    last = send(last, 0, 0, 1)
    return narrow(wide(own) + wide(near) + wide(last))


def scatter_deep(rows):
    count = rows.shape[0] // side
    total = wide(rows[:count])
    for i in range(1, side):
        total = total + wide(send(rows[i * count : (i + 1) * count], 0, -i, 0))
    return total


def normalize(values):
    rows = wide(values)
    radius = jnp.sqrt(jnp.mean(rows * rows, axis=-1, keepdims=True) + epsilon)
    return (rows / radius, radius)


def norm_back(unit_rows, radius, grad_rows):
    inner = jnp.mean(grad_rows * unit_rows, axis=-1, keepdims=True)
    return (grad_rows - unit_rows * inner) / radius


def gelu_value(pre):
    tangent = jnp.tanh(gelu_scale * (pre + cubic_coef * pre * pre * pre))
    return 0.5 * pre * (1.0 + tangent)


def gelu_slope(pre):
    tangent = jnp.tanh(gelu_scale * (pre + cubic_coef * pre * pre * pre))
    return 0.5 * (1.0 + tangent) + 0.5 * pre * (1.0 - tangent * tangent) * gelu_scale * (
        1.0 + 3.0 * cubic_coef * pre * pre
    )


def dot(a, b, dims):
    return lax.dot_general(a, b, (dims, ((), ())), preferred_element_type=jnp.float32)


def gather_targets(cotangent, prev_match, rows):
    peers = lax.axis_size("peer")
    peer = lax.axis_index("peer")
    deep, across = peer // side, peer % side
    width = cotangent.shape[2]
    chunk = width // side
    slots = cotangent[0]
    depth = slots.shape[0] // rows
    cut = [
        lax.dynamic_slice_in_dim(slots, (across + j) % side * chunk, chunk, 1) for j in range(side)
    ]
    mine = [cut[0]] + [send(cut[j], 0, 0, j) for j in range(1, side)]
    held = jnp.concatenate(gather_deep(jnp.concatenate(mine, axis=0)), axis=0)
    blocks = held.reshape(peers * depth, rows, chunk)
    line = jnp.arange(peers, dtype=jnp.int32)
    same = prev_match[:, None] == prev_match[None, :]
    rank = jnp.sum((same & (line[None, :] < line[:, None])).astype(jnp.int32), axis=1)
    source = (deep - line % side + side) % side * side + line // side
    dest = prev_match[source]
    place = (
        ((deep - dest // side + side) % side * side + (across - dest % side + side) % side) * depth
        + rank[source]
    )
    picked = blocks.at[place].get(mode="promise_in_bounds").reshape(peers * rows, chunk)
    after = send(picked, 0, 0, 1)
    before = send(picked, 0, 0, -1)
    half = picked.shape[0] // 2
    far_low = send(after[:half], 0, 0, 1)
    far_high = send(before[half:], 0, 0, -1)
    far = jnp.concatenate([far_low, far_high], axis=0)
    whole = jnp.concatenate([picked, after, far, before], axis=1)
    bulk = whole.shape[0] // side
    turned = jnp.concatenate(
        [
            lax.dynamic_slice_in_dim(whole, (across - j + side) % side * bulk, bulk, 0)
            for j in range(side)
        ],
        axis=0,
    )
    return jnp.concatenate(
        [
            lax.dynamic_slice_in_dim(turned, (across - j + side) % side * chunk, chunk, 1)
            for j in range(side)
        ],
        axis=1,
    )


def shards(hidden, up_weight, down_weight, matching, cotangent):
    peers = lax.axis_size("peer")
    sections = lax.axis_size("section")
    section = lax.axis_index("section")
    rows, width = hidden.shape
    up, down = up_weight[0], down_weight[0]
    part = rows // chains
    prev_match = lax.dynamic_index_in_dim(
        matching[:, :, 0], (section + sections - 1) % sections, 0, keepdims=False
    )
    target = gather_targets(cotangent, prev_match, rows).reshape(peers, rows, width)
    lefts, rights, acts, colds, grads_in = [], [], [], [], []
    for c in range(chains):
        own = hidden[c * part : (c + 1) * part]
        target_c = target[:, c * part : (c + 1) * part].reshape(peers * part, width)
        all_rows = gather_across(jnp.concatenate(gather_deep(own), axis=0))
        first_norm = narrow(normalize(all_rows)[0])
        first_pre = dot(first_norm, up, ((1,), (0,)))
        first_act = narrow(gelu_value(first_pre))
        out = scatter_deep(scatter_across(narrow(dot(first_act, down, ((1,), (0,))))))
        section_out = narrow(wide(own) + out)
        parts = gather_deep(section_out, 1)
        unit_moved, radius_moved = normalize(parts[0])
        second_norm = narrow(normalize(gather_across(jnp.concatenate(parts, axis=0)))[0])
        second_pre = dot(second_norm, up, ((1,), (0,)))
        second_act = narrow(gelu_value(second_pre))
        second_grad = narrow(dot(target_c, down, ((1,), (1,))) * gelu_slope(second_pre))
        second_back = scatter_deep(scatter_across(narrow(dot(second_grad, up, ((1,), (1,))))))
        moved_grad = narrow(
            wide(target_c[:part]) + norm_back(unit_moved, radius_moved, second_back)
        )
        parts = gather_deep(moved_grad, -1)
        back_own = parts[0]
        back = gather_across(jnp.concatenate(parts, axis=0))
        first_grad = narrow(dot(back, down, ((1,), (1,))) * gelu_slope(first_pre))
        first_back = scatter_deep(scatter_across(narrow(dot(first_grad, up, ((1,), (1,))))))
        unit_own, radius_own = normalize(own)
        grads_in.append(narrow(wide(back_own) + norm_back(unit_own, radius_own, first_back)))
        lefts += [first_norm, second_norm]
        rights += [first_grad, second_grad]
        acts += [first_act, second_act]
        colds += [back, target_c]
    grad_up = dot(jnp.concatenate(lefts, axis=0), jnp.concatenate(rights, axis=0), ((0,), (0,)))
    grad_down = dot(jnp.concatenate(acts, axis=0), jnp.concatenate(colds, axis=0), ((0,), (0,)))
    return (narrow(grad_up)[None], narrow(grad_down)[None], jnp.concatenate(grads_in, axis=0))


def solution(mesh):
    in_specs = (
        P(("section", "peer"), None),
        P("section", None, "peer"),
        P("section", "peer", None),
        P(),
        P("section", "peer", None),
    )
    out_specs = (
        P("section", None, "peer"),
        P("section", "peer", None),
        P(("section", "peer"), None),
    )
    return jax.shard_map(shards, mesh=mesh, in_specs=in_specs, out_specs=out_specs, check_vma=False)
```

```python
import math

import jax
import jax.numpy as jnp
from jax import lax
from jax.sharding import PartitionSpec as P

epsilon = 1e-06
gelu_scale = math.sqrt(2.0 / math.pi)
cubic_coef = 0.044715
side = 4
chains = 1


def send(block, sections, deep, across):
    peers = lax.axis_size("peer")
    count = lax.axis_size("section")
    if sections == 0:
        route = [
            (p, (p // side + deep) % side * side + (p % side + across) % side)
            for p in range(peers)
        ]
        return lax.ppermute(block, "peer", route)
    route = [
        (
            s * peers + p,
            (s + sections) % count * peers
            + (p // side + deep) % side * side
            + (p % side + across) % side,
        )
        for s in range(count)
        for p in range(peers)
    ]
    return lax.ppermute(block, ("section", "peer"), route)


def gather_deep(block, sections=0, own=None):
    got = {i: send(block, sections, i, 0) for i in [2, 1, 3]}
    if own is None:
        own = block if sections == 0 else send(block, sections, 0, 0)
    return [own, got[1], got[2], got[3]]


def gather_across(group):
    half = group.shape[0] // 2
    after = send(group, 0, 0, 1)
    before = send(group, 0, 0, -1)
    far_low = send(after[:half], 0, 0, 1)
    far_high = send(before[half:], 0, 0, -1)
    return jnp.concatenate([group, after, far_low, far_high, before], axis=0)


def wide(values):
    return values.astype(jnp.float32)


def narrow(values):
    return values.astype(jnp.bfloat16)


def scatter_across(rows):
    quarter = rows.shape[0] // side
    half = quarter // 2
    own, near, far, last = [rows[j * quarter : (j + 1) * quarter] for j in range(side)]
    low = send(far[:half], 0, 0, -1)
    high = send(far[half:], 0, 0, 1)
    near = jnp.concatenate([narrow(wide(near[:half]) + wide(low)), near[half:]], axis=0)
    last = jnp.concatenate([last[:half], narrow(wide(last[half:]) + wide(high))], axis=0)
    near = send(near, 0, 0, -1)
    last = send(last, 0, 0, 1)
    return narrow(wide(own) + wide(near) + wide(last))


def scatter_deep(rows):
    count = rows.shape[0] // side
    parts = [send(rows[i * count : (i + 1) * count], 0, -i, 0) for i in [2, 1, 3]]
    total = wide(rows[:count])
    for part in parts:
        total = total + wide(part)
    return total


def normalize(values):
    rows = wide(values)
    radius = jnp.sqrt(jnp.mean(rows * rows, axis=-1, keepdims=True) + epsilon)
    return (rows / radius, radius)


def norm_back(unit_rows, radius, grad_rows):
    inner = jnp.mean(grad_rows * unit_rows, axis=-1, keepdims=True)
    return (grad_rows - unit_rows * inner) / radius


def gelu_value(pre):
    tangent = jnp.tanh(gelu_scale * (pre + cubic_coef * pre * pre * pre))
    return 0.5 * pre * (1.0 + tangent)


def gelu_slope(pre):
    tangent = jnp.tanh(gelu_scale * (pre + cubic_coef * pre * pre * pre))
    return 0.5 * (1.0 + tangent) + 0.5 * pre * (1.0 - tangent * tangent) * gelu_scale * (
        1.0 + 3.0 * cubic_coef * pre * pre
    )


def dot(a, b, dims):
    return lax.dot_general(a, b, (dims, ((), ())), preferred_element_type=jnp.float32)


def share_columns(cotangent):
    across = lax.axis_index("peer") % side
    chunk = cotangent.shape[2] // side
    slots = cotangent[0]
    cut = [
        lax.dynamic_slice_in_dim(slots, (across + j) % side * chunk, chunk, 1) for j in range(side)
    ]
    mine = [cut[0]] + [send(cut[j], 0, 0, j) for j in range(1, side)]
    return jnp.concatenate(mine, axis=0)


def pick_targets(held, prev_match, rows):
    peers = lax.axis_size("peer")
    peer = lax.axis_index("peer")
    deep, across = peer // side, peer % side
    chunk = held.shape[1]
    depth = held.shape[0] // peers // rows
    blocks = held.reshape(peers * depth, rows, chunk)
    line = jnp.arange(peers, dtype=jnp.int32)
    same = prev_match[:, None] == prev_match[None, :]
    rank = jnp.sum((same & (line[None, :] < line[:, None])).astype(jnp.int32), axis=1)
    source = (deep - line % side + side) % side * side + line // side
    dest = prev_match[source]
    place = (
        ((deep - dest // side + side) % side * side + (across - dest % side + side) % side) * depth
        + rank[source]
    )
    return blocks.at[place].get(mode="promise_in_bounds").reshape(peers * rows, chunk)


def spread_targets(picked):
    after = send(picked, 0, 0, 1)
    before = send(picked, 0, 0, -1)
    half = picked.shape[0] // 2
    far_low = send(after[:half], 0, 0, 1)
    far_high = send(before[half:], 0, 0, -1)
    return (picked, after, far_low, far_high, before)


def place_targets(picked, after, far_low, far_high, before):
    across = lax.axis_index("peer") % side
    chunk = picked.shape[1]
    far = jnp.concatenate([far_low, far_high], axis=0)
    whole = jnp.concatenate([picked, after, far, before], axis=1)
    bulk = whole.shape[0] // side
    turned = jnp.concatenate(
        [
            lax.dynamic_slice_in_dim(whole, (across - j + side) % side * bulk, bulk, 0)
            for j in range(side)
        ],
        axis=0,
    )
    return jnp.concatenate(
        [
            lax.dynamic_slice_in_dim(turned, (across - j + side) % side * chunk, chunk, 1)
            for j in range(side)
        ],
        axis=1,
    )


def shards(hidden, up_weight, down_weight, matching, cotangent):
    peers = lax.axis_size("peer")
    sections = lax.axis_size("section")
    section = lax.axis_index("section")
    rows, width = hidden.shape
    up, down = up_weight[0], down_weight[0]
    part = rows // chains
    prev_match = lax.dynamic_index_in_dim(
        matching[:, :, 0], (section + sections - 1) % sections, 0, keepdims=False
    )
    lefts, rights, acts, colds, grads_in = [], [], [], [], []
    for c in range(chains):
        own = hidden[c * part : (c + 1) * part]
        unit_own, radius_own = normalize(own)
        parts = gather_deep(own)
        parts[2], slots = lax.optimization_barrier((parts[2], cotangent))
        mine = share_columns(slots)
        group = jnp.concatenate(parts, axis=0)
        group, mine = lax.optimization_barrier((group, mine))
        held = jnp.concatenate(gather_deep(mine), axis=0)
        first_norm = narrow(normalize(gather_across(group))[0])
        first_pre = dot(first_norm, up, ((1,), (0,)))
        first_act = narrow(gelu_value(first_pre))
        partial = narrow(dot(first_act, down, ((1,), (0,))))
        partial, held = lax.optimization_barrier((partial, held))
        picked = pick_targets(held, prev_match, rows)
        summed = scatter_across(partial)
        summed, picked = lax.optimization_barrier((summed, picked))
        pieces = spread_targets(picked)
        section_out = narrow(wide(own) + scatter_deep(summed))
        moved = send(section_out, 1, 0, 0)
        unit_moved, radius_moved = normalize(moved)
        parts = gather_deep(narrow(normalize(section_out)[0]), 1, narrow(unit_moved))
        parts, pieces = lax.optimization_barrier((parts, pieces))
        second_norm = gather_across(jnp.concatenate(parts, axis=0))
        target_c = place_targets(*pieces)
        second_pre = dot(second_norm, up, ((1,), (0,)))
        second_act = narrow(gelu_value(second_pre))
        second_grad = narrow(dot(target_c, down, ((1,), (1,))) * gelu_slope(second_pre))
        second_back = scatter_deep(scatter_across(narrow(dot(second_grad, up, ((1,), (1,))))))
        moved_grad = narrow(
            wide(target_c[:part]) + norm_back(unit_moved, radius_moved, second_back)
        )
        parts = gather_deep(moved_grad, -1)
        back_own = parts[0]
        back = gather_across(jnp.concatenate(parts, axis=0))
        first_grad = narrow(dot(back, down, ((1,), (1,))) * gelu_slope(first_pre))
        first_back = scatter_deep(scatter_across(narrow(dot(first_grad, up, ((1,), (1,))))))
        grads_in.append(narrow(wide(back_own) + norm_back(unit_own, radius_own, first_back)))
        lefts += [first_norm, second_norm]
        rights += [first_grad, second_grad]
        acts += [first_act, second_act]
        colds += [back, target_c]
    grad_up = dot(jnp.concatenate(lefts, axis=0), jnp.concatenate(rights, axis=0), ((0,), (0,)))
    grad_down = dot(jnp.concatenate(acts, axis=0), jnp.concatenate(colds, axis=0), ((0,), (0,)))
    return (narrow(grad_up)[None], narrow(grad_down)[None], jnp.concatenate(grads_in, axis=0))


def solution(mesh):
    in_specs = (
        P(("section", "peer"), None),
        P("section", None, "peer"),
        P("section", "peer", None),
        P(),
        P("section", "peer", None),
    )
    out_specs = (
        P("section", None, "peer"),
        P("section", "peer", None),
        P(("section", "peer"), None),
    )
    return jax.shard_map(shards, mesh=mesh, in_specs=in_specs, out_specs=out_specs, check_vma=False)
```

```python
import math

import jax
import jax.numpy as jnp
from jax import lax
from jax.sharding import PartitionSpec as P

epsilon = 1e-06
gelu_scale = math.sqrt(2.0 / math.pi)
cubic_coef = 0.044715
side = 4
chains = 1


def send(block, sections, deep, across):
    peers = lax.axis_size("peer")
    count = lax.axis_size("section")
    if sections == 0:
        route = [
            (p, (p // side + deep) % side * side + (p % side + across) % side)
            for p in range(peers)
        ]
        return lax.ppermute(block, "peer", route)
    route = [
        (
            s * peers + p,
            (s + sections) % count * peers
            + (p // side + deep) % side * side
            + (p % side + across) % side,
        )
        for s in range(count)
        for p in range(peers)
    ]
    return lax.ppermute(block, ("section", "peer"), route)


def gather_deep(block, sections=0, own=None):
    got = {i: send(block, sections, i, 0) for i in [2, 1, 3]}
    if own is None:
        own = block if sections == 0 else send(block, sections, 0, 0)
    return [own, got[1], got[2], got[3]]


def gather_across(group, beside=None):
    half = group.shape[0] // 2
    after = send(group, 0, 0, 1)
    before = send(group, 0, 0, -1)
    if beside is not None:
        after, before, beside = lax.optimization_barrier((after, before, beside))
    far_low = send(after[:half], 0, 0, 1)
    far_high = send(before[half:], 0, 0, -1)
    rows = jnp.concatenate([group, after, far_low, far_high, before], axis=0)
    return rows if beside is None else (rows, beside)


def wide(values):
    return values.astype(jnp.float32)


def narrow(values):
    return values.astype(jnp.bfloat16)


def scatter_across(rows):
    quarter = rows.shape[0] // side
    half = quarter // 2
    own, near, far, last = [rows[j * quarter : (j + 1) * quarter] for j in range(side)]
    low = send(far[:half], 0, 0, -1)
    high = send(far[half:], 0, 0, 1)
    near = jnp.concatenate([narrow(wide(near[:half]) + wide(low)), near[half:]], axis=0)
    last = jnp.concatenate([last[:half], narrow(wide(last[half:]) + wide(high))], axis=0)
    near = send(near, 0, 0, -1)
    last = send(last, 0, 0, 1)
    return narrow(wide(own) + wide(near) + wide(last))


def scatter_deep(rows):
    count = rows.shape[0] // side
    parts = [send(rows[i * count : (i + 1) * count], 0, -i, 0) for i in [2, 1, 3]]
    total = wide(rows[:count])
    for part in parts:
        total = total + wide(part)
    return total


def normalize(values):
    rows = wide(values)
    radius = jnp.sqrt(jnp.mean(rows * rows, axis=-1, keepdims=True) + epsilon)
    return (rows / radius, radius)


def norm_back(unit_rows, radius, grad_rows):
    inner = jnp.mean(grad_rows * unit_rows, axis=-1, keepdims=True)
    return (grad_rows - unit_rows * inner) / radius


def gelu_value(pre):
    tangent = jnp.tanh(gelu_scale * (pre + cubic_coef * pre * pre * pre))
    return 0.5 * pre * (1.0 + tangent)


def gelu_slope(pre):
    tangent = jnp.tanh(gelu_scale * (pre + cubic_coef * pre * pre * pre))
    return 0.5 * (1.0 + tangent) + 0.5 * pre * (1.0 - tangent * tangent) * gelu_scale * (
        1.0 + 3.0 * cubic_coef * pre * pre
    )


def dot(a, b, dims):
    return lax.dot_general(a, b, (dims, ((), ())), preferred_element_type=jnp.float32)


def share_columns(cotangent):
    across = lax.axis_index("peer") % side
    chunk = cotangent.shape[2] // side
    slots = cotangent[0]
    cut = [
        lax.dynamic_slice_in_dim(slots, (across + j) % side * chunk, chunk, 1) for j in range(side)
    ]
    mine = [cut[0]] + [send(cut[j], 0, 0, j) for j in range(1, side)]
    return jnp.concatenate(mine, axis=0)


def pick_targets(held, prev_match, rows):
    peers = lax.axis_size("peer")
    peer = lax.axis_index("peer")
    deep, across = peer // side, peer % side
    chunk = held.shape[1]
    depth = held.shape[0] // peers // rows
    blocks = held.reshape(peers * depth, rows, chunk)
    line = jnp.arange(peers, dtype=jnp.int32)
    same = prev_match[:, None] == prev_match[None, :]
    rank = jnp.sum((same & (line[None, :] < line[:, None])).astype(jnp.int32), axis=1)
    source = (deep - line % side + side) % side * side + line // side
    dest = prev_match[source]
    place = (
        ((deep - dest // side + side) % side * side + (across - dest % side + side) % side) * depth
        + rank[source]
    )
    return blocks.at[place].get(mode="promise_in_bounds").reshape(peers * rows, chunk)


def spread_targets(picked):
    after = send(picked, 0, 0, 1)
    before = send(picked, 0, 0, -1)
    half = picked.shape[0] // 2
    far_low = send(after[:half], 0, 0, 1)
    far_high = send(before[half:], 0, 0, -1)
    return (picked, after, far_low, far_high, before)


def place_targets(picked, after, far_low, far_high, before):
    across = lax.axis_index("peer") % side
    chunk = picked.shape[1]
    far = jnp.concatenate([far_low, far_high], axis=0)
    whole = jnp.concatenate([picked, after, far, before], axis=1)
    bulk = whole.shape[0] // side
    turned = jnp.concatenate(
        [
            lax.dynamic_slice_in_dim(whole, (across - j + side) % side * bulk, bulk, 0)
            for j in range(side)
        ],
        axis=0,
    )
    return jnp.concatenate(
        [
            lax.dynamic_slice_in_dim(turned, (across - j + side) % side * chunk, chunk, 1)
            for j in range(side)
        ],
        axis=1,
    )


def shards(hidden, up_weight, down_weight, matching, cotangent):
    peers = lax.axis_size("peer")
    sections = lax.axis_size("section")
    section = lax.axis_index("section")
    rows, width = hidden.shape
    up, down = up_weight[0], down_weight[0]
    part = rows // chains
    prev_match = lax.dynamic_index_in_dim(
        matching[:, :, 0], (section + sections - 1) % sections, 0, keepdims=False
    )
    lefts, rights, acts, colds, grads_in = [], [], [], [], []
    for c in range(chains):
        own = hidden[c * part : (c + 1) * part]
        unit_own, radius_own = normalize(own)
        parts = gather_deep(own)
        parts[2], slots = lax.optimization_barrier((parts[2], cotangent))
        mine = share_columns(slots)
        group = jnp.concatenate(parts, axis=0)
        all_rows, mine = gather_across(group, mine)
        held = jnp.concatenate(gather_deep(mine), axis=0)
        first_norm = narrow(normalize(all_rows)[0])
        first_pre = dot(first_norm, up, ((1,), (0,)))
        first_act = narrow(gelu_value(first_pre))
        partial = narrow(dot(first_act, down, ((1,), (0,))))
        partial, held = lax.optimization_barrier((partial, held))
        picked = pick_targets(held, prev_match, rows)
        summed = scatter_across(partial)
        summed, picked = lax.optimization_barrier((summed, picked))
        pieces = spread_targets(picked)
        section_out = narrow(wide(own) + scatter_deep(summed))
        moved = send(section_out, 1, 0, 0)
        unit_moved, radius_moved = normalize(moved)
        parts = gather_deep(narrow(normalize(section_out)[0]), 1, narrow(unit_moved))
        parts, pieces = lax.optimization_barrier((parts, pieces))
        second_norm = gather_across(jnp.concatenate(parts, axis=0))
        target_c = place_targets(*pieces)
        second_pre = dot(second_norm, up, ((1,), (0,)))
        second_act = narrow(gelu_value(second_pre))
        second_grad = narrow(dot(target_c, down, ((1,), (1,))) * gelu_slope(second_pre))
        second_back = scatter_deep(scatter_across(narrow(dot(second_grad, up, ((1,), (1,))))))
        moved_grad = narrow(
            wide(target_c[:part]) + norm_back(unit_moved, radius_moved, second_back)
        )
        parts = gather_deep(moved_grad, -1)
        back_own = parts[0]
        back = gather_across(jnp.concatenate(parts, axis=0))
        first_grad = narrow(dot(back, down, ((1,), (1,))) * gelu_slope(first_pre))
        first_back = scatter_deep(scatter_across(narrow(dot(first_grad, up, ((1,), (1,))))))
        grads_in.append(narrow(wide(back_own) + norm_back(unit_own, radius_own, first_back)))
        lefts += [first_norm, second_norm]
        rights += [first_grad, second_grad]
        acts += [first_act, second_act]
        colds += [back, target_c]
    grad_up = dot(jnp.concatenate(lefts, axis=0), jnp.concatenate(rights, axis=0), ((0,), (0,)))
    grad_down = dot(jnp.concatenate(acts, axis=0), jnp.concatenate(colds, axis=0), ((0,), (0,)))
    return (narrow(grad_up)[None], narrow(grad_down)[None], jnp.concatenate(grads_in, axis=0))


def solution(mesh):
    in_specs = (
        P(("section", "peer"), None),
        P("section", None, "peer"),
        P("section", "peer", None),
        P(),
        P("section", "peer", None),
    )
    out_specs = (
        P("section", None, "peer"),
        P("section", "peer", None),
        P(("section", "peer"), None),
    )
    return jax.shard_map(shards, mesh=mesh, in_specs=in_specs, out_specs=out_specs, check_vma=False)
```
